512 devices in a mesh: ctx: 64 (over z, y_lo, x), head: 8 (over y_hi, core).
Axes of the slice: x: 4, y: 8 (y_hi: 4, y_lo: 2; y = y_hi * 2 + y_lo), z: 8, core: 2. Of those that a mesh axis runs over, the one named last changes fastest.
Arguments:
- queries: bfloat16 [12288, 32, 128], P(('ctx', 'head')), may hold values from -10 to 10
- keys_values: bfloat16 [12288, 8, 256], P(('ctx', 'head')), may hold values from -10 to 10
- span_order: int32 [128], replicated, may hold values from 0 to 127, each once
Outputs:
- attended: bfloat16 [12288, 32, 128], P(('ctx', 'head'))
The draws below stay inside these ranges and needn't reach their ends.
Inputs may be any that keep to these rules, and one draw needn't show every extreme that they name: A permutation: layout span c holds the sequence positions span_order[c] * 96 to span_order[c] * 96 + 95 in order.
All inputs are finite; a program needn't handle non-finite values.
Results may differ from the reference program's by a relative error of at most 0.005.
Values may be sent and summed in bfloat16 or wider, within the bound.
No kernel may reach another device: no remote copies, remote signals or barrier semaphores. Data moves between devices by JAX's collectives and lax.ppermute only.
A program may use at most 64 MiB of HBM per device.

```python
import math
import jax
import jax.numpy as jnp
from jax import lax

HEADS = 32
KV_HEADS = 8
HEAD_DIM = 128
SEQ = 12288
SPAN = 96
N_CTX = 64


def draw_queries(key, part):
    key = jax.random.fold_in(key, 1)
    first, second = jax.random.split(key)
    row_scale = jnp.exp(jax.random.uniform(second, (SEQ, 1, 1), jnp.float32, math.log(0.7), math.log(2.5)))
    base = jnp.clip(jax.random.normal(first, (SEQ, HEADS, HEAD_DIM), jnp.float32), -3.0, 3.0) * row_scale
    return base.astype(jnp.bfloat16)


def draw_keys_values(key, part):
    key = jax.random.fold_in(key, 2)
    first, second, third = jax.random.split(key, 3)
    row_scale = jnp.exp(jax.random.uniform(third, (SEQ, 1, 1), jnp.float32, math.log(0.7), math.log(1.5)))
    values = jnp.clip(jax.random.normal(second, (SEQ, KV_HEADS, HEAD_DIM), jnp.float32), -3.0, 3.0)
    keys_part = jnp.clip(jax.random.normal(first, (SEQ, KV_HEADS, HEAD_DIM), jnp.float32), -3.0, 3.0) * row_scale
    return jnp.concatenate([keys_part, values], axis=2).astype(jnp.bfloat16)


def setup_inputs(seed: int = 0) -> dict:
    keys = jax.random.split(jax.random.key(seed), 4)
    queries = draw_queries(jax.random.fold_in(keys[3], 71), 0)
    keys_values = draw_keys_values(jax.random.fold_in(keys[3], 71), 0)
    span_order = jax.random.permutation(keys[2], 2 * N_CTX).astype(jnp.int32)
    return dict(queries=queries, keys_values=keys_values, span_order=span_order)


def reference(queries, keys_values, span_order):
    rows = jnp.arange(SEQ, dtype=jnp.int32)
    position = (span_order[rows // SPAN] * SPAN + rows % SPAN).astype(jnp.int32)
    group = HEADS // KV_HEADS
    block = math.gcd(SEQ, 512)
    blocks = SEQ // block
    scale = 1.0 / math.sqrt(HEAD_DIM)

    def attend(item):
        kv_index = (item // blocks).astype(jnp.int32)
        start = (item % blocks * block).astype(jnp.int32)
        query_rows = lax.dynamic_slice_in_dim(queries, start, block, 0)
        query_rows = lax.dynamic_slice_in_dim(query_rows, kv_index * group, group, 1)
        paired = lax.dynamic_index_in_dim(keys_values, kv_index, 1, keepdims=False)
        key_part = paired[:, :HEAD_DIM].astype(jnp.float32)
        value_part = paired[:, HEAD_DIM:].astype(jnp.float32)
        scores = jnp.einsum('tgd,sd->gts', query_rows.astype(jnp.float32), key_part) * scale
        query_pos = lax.dynamic_slice_in_dim(position, start, block, 0)
        allowed = position[None, :] <= query_pos[:, None]
        scores = jnp.where(allowed[None], scores, -jnp.inf)
        highest = lax.optimization_barrier(jnp.max(scores, axis=-1, keepdims=True))
        weights = jnp.where(allowed[None], jnp.exp(scores - highest), 0.0)
        denominator = lax.optimization_barrier(jnp.sum(weights, axis=-1))
        rounded = lax.optimization_barrier(weights.astype(jnp.bfloat16)).astype(jnp.float32)
        summed = jnp.einsum('gts,sd->tgd', rounded, value_part)
        return summed / jnp.transpose(denominator)[:, :, None]
    items = jnp.arange(KV_HEADS * blocks, dtype=jnp.int32)
    result = lax.map(attend, items)
    result = result.reshape(KV_HEADS, blocks, block, group, HEAD_DIM)
    result = result.transpose(1, 2, 0, 3, 4).reshape(SEQ, HEADS, HEAD_DIM)
    return result.astype(jnp.bfloat16)
```

```python
import functools
import math

import jax
import jax.numpy as jnp
from jax import lax
from jax.experimental import pallas as pl
from jax.experimental.pallas import tpu as pltpu
from jax.sharding import Mesh, PartitionSpec as P

HEADS = 32
KV_HEADS = 8
GROUP = HEADS // KV_HEADS
HEAD_DIM = 128
HALF = 48
Q_UNITS = 16
K_UNITS = 64
PAIRS = Q_UNITS // 2
CHUNK_UNITS = 8
CHUNK = CHUNK_UNITS * HALF
Q_COLS = GROUP * HEAD_DIM
EXPONENT = math.log2(math.e) / math.sqrt(HEAD_DIM)
LOWEST = -1e30

AXES = ("zh", "zl", "yl", "x", "yh", "core")
SIZES = (4, 2, 2, 4, 4, 2)
HEAD_AXES = ("zl", "yl", "core")
KEY_AXES = ("zh", "yh")


def plan(span_order):
    order = span_order.reshape(4, 2, 2, 4, 2)
    x_is = lax.axis_index("x") == jnp.arange(4)
    zh_is = lax.axis_index("zh") == jnp.arange(4)
    yh = lax.axis_index("yh")
    s_is = (yh // 2) == jnp.arange(2)
    keys = jnp.sum(jnp.where(x_is[:, None], order, 0), axis=3)
    keys = keys[..., None] * 2 + jnp.arange(2)
    keys = jnp.transpose(keys, (0, 3, 4, 1, 2)).reshape(K_UNITS)
    mine = jnp.sum(jnp.where(zh_is[:, None, None, None, None], order, 0), axis=0)
    mine = jnp.sum(jnp.where(s_is, mine, 0), axis=-1)
    queries = jnp.transpose(mine, (2, 0, 1)).reshape(Q_UNITS) * 2 + yh % 2

    def ranked(values):
        n = values.shape[0]
        rank = jnp.sum((values[None, :] < values[:, None]).astype(jnp.int32), axis=1)
        hit = rank[:, None] == jnp.arange(n)[None, :]
        index = jnp.sum(jnp.where(hit, jnp.arange(n)[:, None], 0), axis=0)
        return index, jnp.sum(jnp.where(hit, values[:, None], 0), axis=0)

    k_index, k_sorted = ranked(keys)
    q_index, q_sorted = ranked(queries)
    below = jnp.sum((k_sorted[None, :] < q_sorted[:, None]).astype(jnp.int32), axis=1)
    upto = jnp.sum((k_sorted[None, :] <= q_sorted[:, None]).astype(jnp.int32), axis=1)
    scalars = jnp.concatenate([k_index, q_index, q_sorted, below, upto]).astype(jnp.int32)
    columns = k_sorted[:, None] * HALF + jnp.arange(HALF)[None, :]
    return scalars, columns.reshape(1, K_UNITS * HALF).astype(jnp.int32)


def attend_kernel(scalars, columns, q_ref, kv_ref, out_ref, keys, values, q_pair, top, total):
    k_index, q_index, q_sorted, below, upto = 0, 64, 80, 96, 112
    rows = GROUP * HALF

    values[:, HEAD_DIM:] = jnp.ones((K_UNITS * HALF, HEAD_DIM), jnp.bfloat16)

    def place(unit, _):
        source = pl.multiple_of(scalars[k_index + unit] * HALF, HALF)
        target = pl.multiple_of(unit * HALF, HALF)
        block = kv_ref[pl.ds(source, HALF), :]
        keys[pl.ds(target, HALF), :] = block[:, :HEAD_DIM]
        values[pl.ds(target, HALF), :HEAD_DIM] = block[:, HEAD_DIM:]
        return 0

    lax.fori_loop(0, K_UNITS, place, 0)

    def run_pair(pair, _):
        for side in range(2):
            source = pl.multiple_of(scalars[q_index + 2 * pair + side] * HALF, HALF)
            for g in range(GROUP):
                q_pair[side, g * HALF : (g + 1) * HALF, :] = q_ref[
                    pl.ds(source, HALF), g * HEAD_DIM : (g + 1) * HEAD_DIM
                ]
        top[...] = jnp.full(top.shape, LOWEST, jnp.float32)
        total[...] = jnp.zeros(total.shape, jnp.float32)

        def step(chunk, masked):
            start = pl.multiple_of(chunk * CHUNK, CHUNK)
            key_block = keys[pl.ds(start, CHUNK), :]
            value_block = values[pl.ds(start, CHUNK), :]
            for side in range(2):
                scores = lax.dot_general(
                    q_pair[side],
                    key_block,
                    (((1,), (1,)), ((), ())),
                    preferred_element_type=jnp.float32,
                )
                if masked:
                    row = lax.broadcasted_iota(jnp.int32, (rows, CHUNK), 0) % HALF
                    row = row + scalars[q_sorted + 2 * pair + side] * HALF
                    allowed = columns[:, pl.ds(start, CHUNK)] <= row
                    scores = jnp.where(allowed, scores, LOWEST)
                old_top = top[side]
                new_top = jnp.maximum(old_top, jnp.max(scores, axis=1, keepdims=True))
                weights = jnp.exp2((scores - new_top[:, :1]) * EXPONENT)
                if masked:
                    weights = jnp.where(allowed, weights, 0.0)
                rescale = jnp.exp2((old_top - new_top) * EXPONENT)
                product = jnp.dot(
                    weights.astype(jnp.bfloat16),
                    value_block,
                    preferred_element_type=jnp.float32,
                )
                top[side] = new_top
                total[side] = total[side] * jnp.concatenate([rescale, rescale], axis=1) + product

        free_chunks = scalars[below + 2 * pair] // CHUNK_UNITS
        all_chunks = (scalars[upto + 2 * pair + 1] + CHUNK_UNITS - 1) // CHUNK_UNITS

        def free_step(chunk, _):
            step(chunk, False)
            return 0

        def masked_step(chunk, _):
            step(chunk, True)
            return 0

        lax.fori_loop(0, free_chunks, free_step, 0)
        lax.fori_loop(free_chunks, all_chunks, masked_step, 0)

        lane = lax.broadcasted_iota(jnp.int32, (HALF, HEAD_DIM), 1)
        for side in range(2):
            target = pl.multiple_of(scalars[q_index + 2 * pair + side] * HALF, HALF)
            stats = jnp.zeros((HALF, HEAD_DIM), jnp.float32)
            for g in range(GROUP):
                part = slice(g * HALF, (g + 1) * HALF)
                weight_sum = total[side, part, HEAD_DIM:]
                some = weight_sum > 0.0
                safe = jnp.where(some, weight_sum, 1.0)
                out_ref[pl.ds(target, HALF), g * HEAD_DIM : (g + 1) * HEAD_DIM] = (
                    total[side, part, :HEAD_DIM] / safe
                ).astype(jnp.bfloat16)
                level = jnp.where(some, top[side, part, :] * EXPONENT + jnp.log2(safe), LOWEST)
                high = level.astype(jnp.bfloat16).astype(jnp.float32)
                rest = level - high
                middle = rest.astype(jnp.bfloat16).astype(jnp.float32)
                low = rest - middle
                stats = jnp.where(lane == 3 * g, high, stats)
                stats = jnp.where(lane == 3 * g + 1, middle, stats)
                stats = jnp.where(lane == 3 * g + 2, low, stats)
            out_ref[pl.ds(target, HALF), Q_COLS:] = stats.astype(jnp.bfloat16)
        return 0

    lax.fori_loop(0, PAIRS, run_pair, 0)


def attend(scalars, columns, queries, keys_values):
    vmem = pl.BlockSpec(memory_space=pltpu.VMEM)
    return pl.pallas_call(
        attend_kernel,
        out_shape=jax.ShapeDtypeStruct((Q_UNITS * HALF, Q_COLS + HEAD_DIM), jnp.bfloat16),
        in_specs=[pl.BlockSpec(memory_space=pltpu.SMEM), vmem, vmem, vmem],
        out_specs=vmem,
        scratch_shapes=[
            pltpu.VMEM((K_UNITS * HALF, HEAD_DIM), jnp.bfloat16),
            pltpu.VMEM((K_UNITS * HALF, 2 * HEAD_DIM), jnp.bfloat16),
            pltpu.VMEM((2, GROUP * HALF, HEAD_DIM), jnp.bfloat16),
            pltpu.VMEM((2, GROUP * HALF, HEAD_DIM), jnp.float32),
            pltpu.VMEM((2, GROUP * HALF, 2 * HEAD_DIM), jnp.float32),
        ],
        compiler_params=pltpu.CompilerParams(vmem_limit_bytes=40 * 1024 * 1024),
        cost_estimate=pl.CostEstimate(
            flops=2_400_000_000, bytes_accessed=4_000_000, transcendentals=5_000_000
        ),
        name="attend",
    )(scalars, columns, queries, keys_values)


def combine_kernel(parts_ref, out_ref):
    parts, rows = parts_ref.shape[:2]
    lane = lax.broadcasted_iota(jnp.int32, (rows, HEAD_DIM), 1)
    stats = [parts_ref[p, :, Q_COLS:].astype(jnp.float32) for p in range(parts)]
    for g in range(GROUP):
        chosen = (lane >= 3 * g) & (lane < 3 * g + 3)
        levels = [
            jnp.sum(jnp.where(chosen, s, 0.0), axis=1, keepdims=True) for s in stats
        ]
        highest = functools.reduce(jnp.maximum, levels)
        shares = [jnp.exp2(level - highest) for level in levels]
        inverse = 1.0 / sum(shares)
        columns = slice(g * HEAD_DIM, (g + 1) * HEAD_DIM)
        summed = sum(
            parts_ref[p, :, columns].astype(jnp.float32) * (shares[p] * inverse)
            for p in range(parts)
        )
        out_ref[:, columns] = summed.astype(jnp.bfloat16)


def combine(parts):
    vmem = pl.BlockSpec(memory_space=pltpu.VMEM)
    return pl.pallas_call(
        combine_kernel,
        out_shape=jax.ShapeDtypeStruct((parts.shape[1], Q_COLS), jnp.bfloat16),
        in_specs=[vmem],
        out_specs=vmem,
        name="combine",
    )(parts)


def exchange(blocks, axes):
    return lax.all_to_all(blocks, axes, split_axis=0, concat_axis=0, tiled=True)


def shards(queries, keys_values, span_order):
    rows = queries.shape[0]
    scalars, columns = plan(span_order)
    by_head = queries.reshape(rows, KV_HEADS, Q_COLS)
    packed = jnp.concatenate([by_head, keys_values], axis=2)
    packed = exchange(jnp.transpose(packed, (1, 0, 2)), HEAD_AXES)
    packed = packed.reshape(KV_HEADS * rows, Q_COLS + 2 * HEAD_DIM)
    my_queries = packed[:, :Q_COLS]
    my_keys = packed[:, Q_COLS:]
    all_keys = exchange(jnp.broadcast_to(my_keys[None], (16,) + my_keys.shape), KEY_AXES)
    all_queries = exchange(jnp.broadcast_to(my_queries[None], (4,) + my_queries.shape), "x")
    partial = attend(
        scalars,
        columns,
        all_queries.reshape(Q_UNITS * HALF, Q_COLS),
        all_keys.reshape(K_UNITS * HALF, 2 * HEAD_DIM),
    )
    partial = exchange(partial.reshape(4, KV_HEADS * rows, Q_COLS + HEAD_DIM), "x")
    output = combine(partial)
    output = exchange(output.reshape(KV_HEADS, rows, Q_COLS), HEAD_AXES)
    return jnp.transpose(output, (1, 0, 2)).reshape(rows, HEADS, HEAD_DIM)


def solution(mesh):
    fine = Mesh(mesh.devices.reshape(SIZES), AXES)
    placed = (P(AXES, None, None), P(AXES, None, None), P())
    return jax.shard_map(
        shards,
        mesh=fine,
        in_specs=placed,
        out_specs=P(AXES, None, None),
        check_vma=False,
    )
```

```python
import functools
import math

import jax
import jax.numpy as jnp
from jax import lax
from jax.experimental import pallas as pl
from jax.experimental.pallas import tpu as pltpu
from jax.sharding import Mesh, PartitionSpec as P

HEADS = 32
KV_HEADS = 8
GROUP = HEADS // KV_HEADS
HEAD_DIM = 128
SPAN = 96
QUARTER = 24
UNIT = 48
Q_HEADS = 2
SPANS = 32
KEYS = SPANS * SPAN
Q_ROWS = SPANS * UNIT
TOGETHER = 4
GROUP_ROWS = TOGETHER * Q_HEADS * UNIT
PARTS = 2
PART_ROWS = GROUP_ROWS // PARTS
WIDE = 512
NARROW = 256
Q_COLS = Q_HEADS * HEAD_DIM
BLOCK_ROWS = 384
STAT_ROWS = 32
EXPONENT = math.log2(math.e) / math.sqrt(HEAD_DIM)
LOWEST = -1e30

AXES = ("zh", "zl", "yl", "x", "yh", "core")
SIZES = (4, 2, 2, 4, 4, 2)
HEAD_AXES = ("zh", "yh")
QUERY_AXES = ("zl", "yl")

K_INDEX, Q_INDEX, Q_SORTED, BELOW, UPTO, CORE = 0, 32, 64, 96, 128, 160


def ranked(values):
    n = values.shape[0]
    rank = jnp.sum((values[None, :] < values[:, None]).astype(jnp.int32), axis=1)
    hit = rank[:, None] == jnp.arange(n)[None, :]
    index = jnp.sum(jnp.where(hit, jnp.arange(n)[:, None], 0), axis=0)
    return index, jnp.sum(jnp.where(hit, values[:, None], 0), axis=0)


def plan(span_order):
    order = span_order.reshape(4, 2, 2, 4, 2)
    x_is = lax.axis_index("x") == jnp.arange(4)
    zl_is = lax.axis_index("zl") == jnp.arange(2)
    yl_is = lax.axis_index("yl") == jnp.arange(2)
    near = zl_is[:, None, None, None] & yl_is[:, None, None]
    keys = jnp.sum(jnp.where(near, order, 0), axis=(1, 2))
    keys = jnp.transpose(keys, (1, 0, 2)).reshape(SPANS)
    queries = jnp.sum(jnp.where(x_is[:, None], order, 0), axis=3)
    queries = jnp.transpose(queries, (1, 2, 0, 3)).reshape(SPANS)
    k_index, k_sorted = ranked(keys)
    q_index, q_sorted = ranked(queries)
    below = jnp.sum((k_sorted[None, :] < q_sorted[:, None]).astype(jnp.int32), axis=1)
    upto = jnp.sum((k_sorted[None, :] <= q_sorted[:, None]).astype(jnp.int32), axis=1)
    core = jnp.full((SPANS,), lax.axis_index("core"), jnp.int32)
    scalars = jnp.concatenate([k_index, q_index, q_sorted, below, upto, core])
    row = jnp.arange(SPAN, dtype=jnp.int32)
    half, place = row // UNIT, row % UNIT
    offset = half * QUARTER + place + (place // QUARTER) * QUARTER
    columns = k_sorted[:, None] * SPAN + offset[None, :]
    return scalars.astype(jnp.int32), columns.reshape(1, KEYS).astype(jnp.int32)


def attend_kernel(
    scalars, columns, q_ref, kv_ref, out_ref,
    keys, values, q_group, q_position, scores, top, total, stats,
):
    values[:, HEAD_DIM:] = jnp.ones((KEYS, HEAD_DIM), jnp.bfloat16)

    def place(rank, _):
        for core in range(2):
            source = (core * SPANS + scalars[K_INDEX + rank]) * UNIT
            target = (2 * rank + core) * UNIT
            block = kv_ref[pl.ds(pl.multiple_of(source, UNIT), UNIT), :]
            target = pl.ds(pl.multiple_of(target, UNIT), UNIT)
            keys[target, :] = block[:, :HEAD_DIM]
            values[target, :HEAD_DIM] = block[:, HEAD_DIM:]
        return 0

    lax.fori_loop(0, SPANS, place, 0)

    row = lax.broadcasted_iota(jnp.int32, (UNIT, HEAD_DIM), 0)
    offset = row + jnp.where(row >= QUARTER, QUARTER, 0) + scalars[CORE] * QUARTER
    lane = lax.broadcasted_iota(jnp.int32, (UNIT, HEAD_DIM), 1)
    part_rows = [slice(p * PART_ROWS, (p + 1) * PART_ROWS) for p in range(PARTS)]

    def run_group(group, _):
        first = group * TOGETHER
        for u in range(TOGETHER):
            source = pl.multiple_of(scalars[Q_INDEX + first + u] * UNIT, UNIT)
            position = scalars[Q_SORTED + first + u] * SPAN + offset
            for g in range(Q_HEADS):
                to = slice((u * Q_HEADS + g) * UNIT, (u * Q_HEADS + g + 1) * UNIT)
                q_group[to, :] = q_ref[
                    pl.ds(source, UNIT), g * HEAD_DIM : (g + 1) * HEAD_DIM
                ]
                q_position[to, :] = position
        top[...] = jnp.full(top.shape, LOWEST, jnp.float32)
        total[...] = jnp.zeros(total.shape, jnp.float32)

        def score(start, width, masked):
            key_block = keys[pl.ds(start, width), :]
            for rows in part_rows:
                block = lax.dot_general(
                    q_group[rows, :],
                    key_block,
                    (((1,), (1,)), ((), ())),
                    preferred_element_type=jnp.float32,
                )
                tiles = []
                for t in range(width // HEAD_DIM):
                    tile = block[:, t * HEAD_DIM : (t + 1) * HEAD_DIM]
                    at = pl.multiple_of(start + t * HEAD_DIM, HEAD_DIM)
                    if masked:
                        allowed = columns[:, pl.ds(at, HEAD_DIM)] <= q_position[rows, :]
                        tile = jnp.where(allowed, tile, LOWEST)
                    scores[rows, pl.ds(at, HEAD_DIM)] = tile
                    tiles.append(tile)
                top[rows, :] = functools.reduce(jnp.maximum, tiles, top[rows, :])

        def weigh(start, width):
            value_block = values[pl.ds(start, width), :]
            for rows in part_rows:
                highest = top[rows, :]
                tiles = []
                for t in range(width // HEAD_DIM):
                    at = pl.multiple_of(start + t * HEAD_DIM, HEAD_DIM)
                    tile = (scores[rows, pl.ds(at, HEAD_DIM)] - highest) * EXPONENT
                    tiles.append(jnp.exp2(tile).astype(jnp.bfloat16))
                total[rows, :] += jnp.dot(
                    jnp.concatenate(tiles, axis=1),
                    value_block,
                    preferred_element_type=jnp.float32,
                )

        free = scalars[BELOW + first] * SPAN // WIDE
        ends = (scalars[UPTO + first + TOGETHER - 1] * SPAN + NARROW - 1) // NARROW

        def free_step(step, _):
            score(pl.multiple_of(step * WIDE, WIDE), WIDE, False)
            return 0

        def masked_step(step, _):
            score(pl.multiple_of(step * NARROW, NARROW), NARROW, True)
            return 0

        def wide_step(step, _):
            weigh(pl.multiple_of(step * WIDE, WIDE), WIDE)
            return 0

        def narrow_step(step, _):
            weigh(pl.multiple_of(step * NARROW, NARROW), NARROW)
            return 0

        ratio = WIDE // NARROW
        lax.fori_loop(0, free, free_step, 0)
        lax.fori_loop(free * ratio, ends, masked_step, 0)
        top[...] = jnp.broadcast_to(jnp.max(top[...], axis=1, keepdims=True), top.shape)
        lax.fori_loop(0, ends // ratio, wide_step, 0)
        lax.fori_loop(ends // ratio * ratio, ends, narrow_step, 0)

        for u in range(TOGETHER):
            unit = scalars[Q_INDEX + first + u]
            block, within = unit // 8, unit % 8
            target = block * (BLOCK_ROWS + STAT_ROWS) + within * UNIT
            target = pl.ds(pl.multiple_of(target, 16), UNIT)
            packed = jnp.zeros((UNIT, HEAD_DIM), jnp.float32)
            for g in range(Q_HEADS):
                part = slice((u * Q_HEADS + g) * UNIT, (u * Q_HEADS + g + 1) * UNIT)
                weight_sum = total[part, HEAD_DIM:]
                highest = top[part, :]
                some = (highest > LOWEST) & (weight_sum > 0.0)
                safe = jnp.where(some, weight_sum, 1.0)
                out_ref[target, g * HEAD_DIM : (g + 1) * HEAD_DIM] = (
                    total[part, :HEAD_DIM] / safe
                ).astype(jnp.bfloat16)
                level = jnp.where(some, highest * EXPONENT + jnp.log2(safe), LOWEST)
                high = level.astype(jnp.bfloat16).astype(jnp.float32)
                rest = level - high
                middle = rest.astype(jnp.bfloat16).astype(jnp.float32)
                low = rest - middle
                packed = jnp.where(lane == 3 * g, high, packed)
                packed = jnp.where(lane == 3 * g + 1, middle, packed)
                packed = jnp.where(lane == 3 * g + 2, low, packed)
            stats[pl.ds(pl.multiple_of(unit * UNIT, UNIT), UNIT), :] = packed.astype(
                jnp.bfloat16
            )
        return 0

    lax.fori_loop(0, SPANS // TOGETHER, run_group, 0)

    pick = (
        lax.broadcasted_iota(jnp.int32, (16, HEAD_DIM), 0)
        == lax.broadcasted_iota(jnp.int32, (16, HEAD_DIM), 1)
    ).astype(jnp.bfloat16)
    for block in range(Q_ROWS // BLOCK_ROWS):
        turned = lax.dot_general(
            pick,
            stats[block * BLOCK_ROWS : (block + 1) * BLOCK_ROWS, :],
            (((1,), (1,)), ((), ())),
            preferred_element_type=jnp.float32,
        ).astype(jnp.bfloat16)
        at = block * (BLOCK_ROWS + STAT_ROWS) + BLOCK_ROWS
        out_ref[at : at + 16, :] = turned[:, :Q_COLS]
        out_ref[at + 16 : at + 32, :HEAD_DIM] = turned[:, Q_COLS:]
        out_ref[at + 16 : at + 32, HEAD_DIM:] = jnp.zeros((16, HEAD_DIM), jnp.bfloat16)


def attend(scalars, columns, queries, keys_values):
    vmem = pl.BlockSpec(memory_space=pltpu.VMEM)
    blocks = Q_ROWS // BLOCK_ROWS
    return pl.pallas_call(
        attend_kernel,
        out_shape=jax.ShapeDtypeStruct((blocks * (BLOCK_ROWS + STAT_ROWS), Q_COLS), jnp.bfloat16),
        in_specs=[pl.BlockSpec(memory_space=pltpu.SMEM), vmem, vmem, vmem],
        out_specs=vmem,
        scratch_shapes=[
            pltpu.VMEM((KEYS, HEAD_DIM), jnp.bfloat16),
            pltpu.VMEM((KEYS, 2 * HEAD_DIM), jnp.bfloat16),
            pltpu.VMEM((GROUP_ROWS, HEAD_DIM), jnp.bfloat16),
            pltpu.VMEM((GROUP_ROWS, HEAD_DIM), jnp.int32),
            pltpu.VMEM((GROUP_ROWS, KEYS), jnp.float32),
            pltpu.VMEM((GROUP_ROWS, HEAD_DIM), jnp.float32),
            pltpu.VMEM((GROUP_ROWS, 2 * HEAD_DIM), jnp.float32),
            pltpu.VMEM((Q_ROWS, HEAD_DIM), jnp.bfloat16),
        ],
        compiler_params=pltpu.CompilerParams(vmem_limit_bytes=40 * 1024 * 1024),
        cost_estimate=pl.CostEstimate(
            flops=2_400_000_000, bytes_accessed=4_000_000, transcendentals=5_000_000
        ),
        name="attend",
    )(scalars, columns, queries, keys_values)


def combine_kernel(parts_ref, out_ref):
    parts = parts_ref.shape[0]
    row = lax.broadcasted_iota(jnp.int32, (16, Q_COLS), 0)
    head = lax.broadcasted_iota(jnp.int32, (16, Q_COLS), 1) // HEAD_DIM
    spread = ((row >= 3 * head) & (row < 3 * head + 3)).astype(jnp.bfloat16)
    levels = []
    for p in range(parts):
        at = BLOCK_ROWS
        turned = jnp.concatenate(
            [parts_ref[p, at : at + 16, :], parts_ref[p, at + 16 : at + 32, :HEAD_DIM]],
            axis=1,
        )
        levels.append(
            lax.dot_general(
                turned,
                spread,
                (((0,), (0,)), ((), ())),
                preferred_element_type=jnp.float32,
            )
        )
    highest = functools.reduce(jnp.maximum, levels)
    shares = [jnp.exp2(level - highest) for level in levels]
    summed = sum(
        parts_ref[p, :BLOCK_ROWS, :].astype(jnp.float32) * shares[p] for p in range(parts)
    )
    out_ref[...] = (summed / sum(shares)).astype(jnp.bfloat16)


def combine(parts):
    vmem = pl.BlockSpec(memory_space=pltpu.VMEM)
    return pl.pallas_call(
        combine_kernel,
        out_shape=jax.ShapeDtypeStruct((BLOCK_ROWS, Q_COLS), jnp.bfloat16),
        in_specs=[vmem],
        out_specs=vmem,
        name="combine",
    )(parts)


def exchange(blocks, axes):
    return lax.all_to_all(blocks, axes, split_axis=0, concat_axis=0, tiled=True)


def shards(queries, keys_values, span_order):
    rows = queries.shape[0]
    scalars, columns = plan(span_order)
    by_head = queries.reshape(rows, HEADS // Q_HEADS, Q_COLS)
    packed = jnp.concatenate([by_head, jnp.repeat(keys_values, 2, axis=1)], axis=2)
    packed = exchange(jnp.transpose(packed, (1, 0, 2)), HEAD_AXES)
    packed = packed.reshape(BLOCK_ROWS, Q_COLS + 2 * HEAD_DIM)
    my_queries = packed[:, :Q_COLS]
    my_keys = packed[:, Q_COLS:]
    some_keys = exchange(jnp.broadcast_to(my_keys[None], (4,) + my_keys.shape), "x")
    all_queries = exchange(
        jnp.broadcast_to(my_queries[None], (4,) + my_queries.shape), QUERY_AXES
    )
    all_keys = lax.all_gather(some_keys, "core", axis=0, tiled=True)
    partial = attend(
        scalars,
        columns,
        all_queries.reshape(Q_ROWS, Q_COLS),
        all_keys.reshape(KEYS, 2 * HEAD_DIM),
    )
    partial = partial.reshape(4, BLOCK_ROWS + STAT_ROWS, Q_COLS)
    output = combine(exchange(partial, QUERY_AXES))
    output = exchange(output.reshape(HEADS // Q_HEADS, rows, Q_COLS), HEAD_AXES)
    return jnp.transpose(output, (1, 0, 2)).reshape(rows, HEADS, HEAD_DIM)


def solution(mesh):
    fine = Mesh(mesh.devices.reshape(SIZES), AXES)
    placed = (P(AXES, None, None), P(AXES, None, None), P())
    return jax.shard_map(
        shards,
        mesh=fine,
        in_specs=placed,
        out_specs=P(AXES, None, None),
        check_vma=False,
    )
```

```python
import functools
import math

import jax
import jax.numpy as jnp
from jax import lax
from jax.experimental import pallas as pl
from jax.experimental.pallas import tpu as pltpu
from jax.sharding import Mesh, PartitionSpec as P

HEADS = 32
KV_HEADS = 8
GROUP = HEADS // KV_HEADS
HEAD_DIM = 128
SPAN = 96
QUARTER = 24
UNIT = 48
K_SPANS = 32
KEYS = K_SPANS * SPAN
Q_UNITS = 16
Q_ROWS = Q_UNITS * UNIT
TOGETHER = 4
GROUP_ROWS = TOGETHER * GROUP * UNIT
PARTS = 2
PART_ROWS = GROUP_ROWS // PARTS
CHUNK = 1024
CHUNKS = KEYS // CHUNK
Q_COLS = GROUP * HEAD_DIM
BLOCK_ROWS = 192
STAT_ROWS = 16
EXPONENT = math.log2(math.e) / math.sqrt(HEAD_DIM)
LOWEST = -1e30

AXES = ("z2", "z1", "zl", "yl", "x", "y2", "y1", "core")
SIZES = (2, 2, 2, 2, 4, 2, 2, 2)
HEAD_AXES = ("zl", "yl", "y1")
QUERY_AXES = ("x",)
KEY_AXES = ("z2", "z1", "zl", "yl", "y2", "y1")

K_INDEX, Q_INDEX, Q_SORTED, BELOW, UPTO, HERE = 0, 32, 48, 64, 80, 96


def ranked(values):
    n = values.shape[0]
    rank = jnp.sum((values[None, :] < values[:, None]).astype(jnp.int32), axis=1)
    hit = rank[:, None] == jnp.arange(n)[None, :]
    index = jnp.sum(jnp.where(hit, jnp.arange(n)[:, None], 0), axis=0)
    return index, jnp.sum(jnp.where(hit, values[:, None], 0), axis=0)


def plan(span_order, place):
    order = span_order.reshape(4, 4, 4, 2)
    x_is = place["x"] == jnp.arange(4)
    far = place["z2"] * 2 + place["z1"] == jnp.arange(4)
    half = place["y2"] == jnp.arange(2)
    keys = jnp.sum(jnp.where(x_is[:, None], order, 0), axis=2).reshape(K_SPANS)
    mine = far[:, None, None, None] & half
    queries = jnp.sum(jnp.where(mine, order, 0), axis=(0, 3))
    source = (place["x"] - jnp.arange(4)) % 4
    picked = source[:, None] == jnp.arange(4)
    queries = jnp.sum(jnp.where(picked[:, None, :], queries[None], 0), axis=2)
    queries = queries.reshape(Q_UNITS)
    k_index, k_sorted = ranked(keys)
    q_index, q_sorted = ranked(queries)
    below = jnp.sum((k_sorted[None, :] < q_sorted[:, None]).astype(jnp.int32), axis=1)
    upto = jnp.sum((k_sorted[None, :] <= q_sorted[:, None]).astype(jnp.int32), axis=1)
    here = jnp.full((Q_UNITS,), place["core"] * 4 + place["x"], jnp.int32)
    scalars = jnp.concatenate([k_index, q_index, q_sorted, below, upto, here])
    row = jnp.arange(SPAN, dtype=jnp.int32)
    core = jnp.where(row < UNIT, place["core"], 1 - place["core"])
    within = row % UNIT
    offset = core * QUARTER + within + (within // QUARTER) * QUARTER
    columns = k_sorted[:, None] * SPAN + offset[None, :]
    return scalars.astype(jnp.int32), columns.reshape(CHUNKS, 1, CHUNK).astype(jnp.int32)


def attend_kernel(
    scalars, columns, q0_ref, q1_ref, q2_ref, q3_ref, own_ref, other_ref, out_ref,
    q_ref, sorted_kv, keys_t, values, q_group, q_position, scores, top, total, stats,
):
    for block, block_ref in enumerate((q0_ref, q1_ref, q2_ref, q3_ref)):
        q_ref[block * BLOCK_ROWS : (block + 1) * BLOCK_ROWS, :] = block_ref[...]

    def place(rank, _):
        source = pl.multiple_of(scalars[K_INDEX + rank] * UNIT, UNIT)
        for half, kv_ref in enumerate((own_ref, other_ref)):
            target = pl.ds(pl.multiple_of((2 * rank + half) * UNIT, UNIT), UNIT)
            sorted_kv[target, :] = kv_ref[pl.ds(source, UNIT), :]
        return 0

    lax.fori_loop(0, K_SPANS, place, 0)
    for chunk in range(CHUNKS):
        rows = slice(chunk * CHUNK, (chunk + 1) * CHUNK)
        keys_t[chunk] = sorted_kv[rows, :HEAD_DIM].T
        values[chunk, :, :HEAD_DIM] = sorted_kv[rows, HEAD_DIM:]
        values[chunk, :, HEAD_DIM:] = jnp.ones((CHUNK, HEAD_DIM), jnp.bfloat16)

    row = lax.broadcasted_iota(jnp.int32, (UNIT, HEAD_DIM), 0)
    offset = row + jnp.where(row >= QUARTER, QUARTER, 0) + scalars[HERE] // 4 * QUARTER
    lane = lax.broadcasted_iota(jnp.int32, (UNIT, HEAD_DIM), 1)
    part_rows = [slice(p * PART_ROWS, (p + 1) * PART_ROWS) for p in range(PARTS)]

    def run_group(group, _):
        first = group * TOGETHER
        for u in range(TOGETHER):
            source = pl.multiple_of(scalars[Q_INDEX + first + u] * UNIT, UNIT)
            position = scalars[Q_SORTED + first + u] * SPAN + offset
            for g in range(GROUP):
                to = slice((u * GROUP + g) * UNIT, (u * GROUP + g + 1) * UNIT)
                q_group[to, :] = q_ref[
                    pl.ds(source, UNIT), g * HEAD_DIM : (g + 1) * HEAD_DIM
                ]
                q_position[to, :] = position
        top[...] = jnp.full(top.shape, LOWEST, jnp.float32)
        total[...] = jnp.zeros(total.shape, jnp.float32)

        def score(chunk, masked):
            for rows in part_rows:
                block = jnp.dot(
                    q_group[rows, :], keys_t[chunk], preferred_element_type=jnp.float32
                )
                if masked:
                    position = q_position[rows, :]
                    tiles = [
                        jnp.where(
                            columns[chunk, :, t : t + HEAD_DIM] <= position,
                            block[:, t : t + HEAD_DIM],
                            LOWEST,
                        )
                        for t in range(0, CHUNK, HEAD_DIM)
                    ]
                    block = jnp.concatenate(tiles, axis=1)
                else:
                    tiles = [block[:, t : t + HEAD_DIM] for t in range(0, CHUNK, HEAD_DIM)]
                scores[chunk, rows, :] = block
                top[rows, :] = functools.reduce(jnp.maximum, tiles, top[rows, :])

        def weigh(chunk):
            for rows in part_rows:
                highest = top[rows, :]
                tiles = [
                    jnp.exp2((scores[chunk, rows, t : t + HEAD_DIM] - highest) * EXPONENT)
                    for t in range(0, CHUNK, HEAD_DIM)
                ]
                total[rows, :] += jnp.dot(
                    jnp.concatenate(tiles, axis=1).astype(jnp.bfloat16),
                    values[chunk],
                    preferred_element_type=jnp.float32,
                )

        free = scalars[BELOW + first] * SPAN // CHUNK
        ends = (scalars[UPTO + first + TOGETHER - 1] * SPAN + CHUNK - 1) // CHUNK

        def free_step(chunk, _):
            score(chunk, False)
            return 0

        def masked_step(chunk, _):
            score(chunk, True)
            return 0

        def weigh_step(chunk, _):
            weigh(chunk)
            return 0

        lax.fori_loop(0, free, free_step, 0)
        lax.fori_loop(free, ends, masked_step, 0)
        top[...] = jnp.broadcast_to(jnp.max(top[...], axis=1, keepdims=True), top.shape)
        lax.fori_loop(0, ends, weigh_step, 0)

        for u in range(TOGETHER):
            unit = scalars[Q_INDEX + first + u]
            block, within = (scalars[HERE] - unit // 4) % 4, unit % 4
            target = block * (BLOCK_ROWS + STAT_ROWS) + within * UNIT
            target = pl.ds(pl.multiple_of(target, 16), UNIT)
            packed = jnp.zeros((UNIT, HEAD_DIM), jnp.float32)
            for g in range(GROUP):
                part = slice((u * GROUP + g) * UNIT, (u * GROUP + g + 1) * UNIT)
                weight_sum = total[part, HEAD_DIM:]
                highest = top[part, :]
                some = (highest > LOWEST) & (weight_sum > 0.0)
                safe = jnp.where(some, weight_sum, 1.0)
                out_ref[target, g * HEAD_DIM : (g + 1) * HEAD_DIM] = (
                    total[part, :HEAD_DIM] / safe
                ).astype(jnp.bfloat16)
                level = jnp.where(some, highest * EXPONENT + jnp.log2(safe), LOWEST)
                high = level.astype(jnp.bfloat16).astype(jnp.float32)
                rest = level - high
                middle = rest.astype(jnp.bfloat16).astype(jnp.float32)
                low = rest - middle
                packed = jnp.where(lane == 3 * g, high, packed)
                packed = jnp.where(lane == 3 * g + 1, middle, packed)
                packed = jnp.where(lane == 3 * g + 2, low, packed)
            target = pl.ds(pl.multiple_of(block * BLOCK_ROWS + within * UNIT, UNIT), UNIT)
            stats[target, :] = packed.astype(jnp.bfloat16)
        return 0

    lax.fori_loop(0, Q_UNITS // TOGETHER, run_group, 0)

    pick = (
        lax.broadcasted_iota(jnp.int32, (16, HEAD_DIM), 0)
        == lax.broadcasted_iota(jnp.int32, (16, HEAD_DIM), 1)
    ).astype(jnp.bfloat16)
    for block in range(Q_ROWS // BLOCK_ROWS):
        turned = lax.dot_general(
            pick,
            stats[block * BLOCK_ROWS : (block + 1) * BLOCK_ROWS, :],
            (((1,), (1,)), ((), ())),
            preferred_element_type=jnp.float32,
        ).astype(jnp.bfloat16)
        at = block * (BLOCK_ROWS + STAT_ROWS) + BLOCK_ROWS
        out_ref[at : at + STAT_ROWS, :BLOCK_ROWS] = turned
        out_ref[at : at + STAT_ROWS, BLOCK_ROWS:] = jnp.zeros(
            (STAT_ROWS, Q_COLS - BLOCK_ROWS), jnp.bfloat16
        )


def attend(scalars, columns, *arrays):
    vmem = pl.BlockSpec(memory_space=pltpu.VMEM)
    blocks = Q_ROWS // BLOCK_ROWS
    return pl.pallas_call(
        attend_kernel,
        out_shape=jax.ShapeDtypeStruct((blocks * (BLOCK_ROWS + STAT_ROWS), Q_COLS), jnp.bfloat16),
        in_specs=[pl.BlockSpec(memory_space=pltpu.SMEM)] + [vmem] * 7,
        out_specs=vmem,
        scratch_shapes=[
            pltpu.VMEM((Q_ROWS, Q_COLS), jnp.bfloat16),
            pltpu.VMEM((KEYS, 2 * HEAD_DIM), jnp.bfloat16),
            pltpu.VMEM((CHUNKS, HEAD_DIM, CHUNK), jnp.bfloat16),
            pltpu.VMEM((CHUNKS, CHUNK, 2 * HEAD_DIM), jnp.bfloat16),
            pltpu.VMEM((GROUP_ROWS, HEAD_DIM), jnp.bfloat16),
            pltpu.VMEM((GROUP_ROWS, HEAD_DIM), jnp.int32),
            pltpu.VMEM((CHUNKS, GROUP_ROWS, CHUNK), jnp.float32),
            pltpu.VMEM((GROUP_ROWS, HEAD_DIM), jnp.float32),
            pltpu.VMEM((GROUP_ROWS, 2 * HEAD_DIM), jnp.float32),
            pltpu.VMEM((Q_ROWS, HEAD_DIM), jnp.bfloat16),
        ],
        compiler_params=pltpu.CompilerParams(vmem_limit_bytes=40 * 1024 * 1024),
        cost_estimate=pl.CostEstimate(
            flops=2_400_000_000, bytes_accessed=4_000_000, transcendentals=5_000_000
        ),
        name="attend",
    )(scalars, columns, *arrays)


def combine_kernel(parts_ref, out_ref):
    parts = parts_ref.shape[0]
    row = lax.broadcasted_iota(jnp.int32, (16, Q_COLS), 0)
    head = lax.broadcasted_iota(jnp.int32, (16, Q_COLS), 1) // HEAD_DIM
    spread = ((row >= 3 * head) & (row < 3 * head + 3)).astype(jnp.bfloat16)
    levels = []
    for p in range(parts):
        turned = parts_ref[p, BLOCK_ROWS:, :BLOCK_ROWS]
        levels.append(
            lax.dot_general(
                turned,
                spread,
                (((0,), (0,)), ((), ())),
                preferred_element_type=jnp.float32,
            )
        )
    highest = functools.reduce(jnp.maximum, levels)
    shares = [jnp.exp2(level - highest) for level in levels]
    summed = sum(
        parts_ref[p, :BLOCK_ROWS, :].astype(jnp.float32) * shares[p] for p in range(parts)
    )
    out_ref[...] = (summed / sum(shares)).astype(jnp.bfloat16)


def combine(parts):
    vmem = pl.BlockSpec(memory_space=pltpu.VMEM)
    return pl.pallas_call(
        combine_kernel,
        out_shape=jax.ShapeDtypeStruct((BLOCK_ROWS, Q_COLS), jnp.bfloat16),
        in_specs=[vmem],
        out_specs=vmem,
        name="combine",
    )(parts)


def exchange(blocks, axes):
    return lax.all_to_all(blocks, axes, split_axis=0, concat_axis=0, tiled=True)


def spread(blocks, axes, chosen):
    sizes = [SIZES[AXES.index(a)] for a in axes]
    lead = [n if a in chosen else 1 for a, n in zip(axes, sizes)]
    shape = blocks.shape[1:]
    blocks = jnp.broadcast_to(blocks.reshape(*lead, *shape), (*sizes, *shape))
    return blocks.reshape(math.prod(sizes), *shape)


def turn(block, axis, step):
    size = SIZES[AXES.index(axis)]
    return lax.ppermute(block, axis, [(i, (i + step) % size) for i in range(size)])


def shards(queries, keys_values, span_order):
    rows = queries.shape[0]
    scalars, columns = plan(span_order, {a: lax.axis_index(a) for a in AXES})
    by_head = jnp.transpose(queries.reshape(rows, KV_HEADS, Q_COLS), (1, 0, 2))
    mine = exchange(by_head, HEAD_AXES).reshape(BLOCK_ROWS, Q_COLS)
    own = jnp.transpose(keys_values, (1, 0, 2))
    mine, own = lax.optimization_barrier((mine, own))
    own = spread(own, KEY_AXES, HEAD_AXES)
    own = exchange(own, KEY_AXES).reshape(KEYS // 2, 2 * HEAD_DIM)
    gathered = [mine] + [turn(mine, "x", step) for step in range(1, 4)]
    own, *gathered = lax.optimization_barrier((own, *gathered))
    other = turn(own, "core", 1)
    partial = attend(scalars, columns, *gathered, own, other)
    partial = partial.reshape(4, BLOCK_ROWS + STAT_ROWS, Q_COLS)
    output = combine(exchange(partial, QUERY_AXES))
    output = exchange(output.reshape(KV_HEADS, rows, Q_COLS), HEAD_AXES)
    return jnp.transpose(output, (1, 0, 2)).reshape(rows, HEADS, HEAD_DIM)


def solution(mesh):
    fine = Mesh(mesh.devices.reshape(SIZES), AXES)
    placed = (P(AXES, None, None), P(AXES, None, None), P())
    return jax.shard_map(
        shards,
        mesh=fine,
        in_specs=placed,
        out_specs=P(AXES, None, None),
        check_vma=False,
    )
```

```python
import functools
import math

import jax
import jax.numpy as jnp
from jax import lax
from jax.experimental import pallas as pl
from jax.experimental.pallas import tpu as pltpu
from jax.sharding import Mesh, PartitionSpec as P

HEADS = 32
KV_HEADS = 8
GROUP = HEADS // KV_HEADS
HEAD_DIM = 128
SPAN = 96
QUARTER = 24
UNIT = 48
K_SPANS = 32
KEYS = K_SPANS * SPAN
Q_UNITS = 16
Q_ROWS = Q_UNITS * UNIT
TOGETHER = 4
GROUP_ROWS = TOGETHER * GROUP * UNIT
PARTS = 4
PART_ROWS = GROUP_ROWS // PARTS
CHUNK = 768
CHUNKS = KEYS // CHUNK
Q_COLS = GROUP * HEAD_DIM
BLOCK_ROWS = 192
STAT_ROWS = 16
EXPONENT = math.log2(math.e) / math.sqrt(HEAD_DIM)
LOWEST = -1e30

AXES = ("z2", "z1", "zl", "yl", "x", "y2", "y1", "core")
SIZES = (2, 2, 2, 2, 4, 2, 2, 2)
HEAD_AXES = ("zl", "yl", "y1")
QUERY_AXES = ("x",)
KEY_AXES = ("z2", "z1", "zl", "yl", "y2", "y1")

K_INDEX, Q_INDEX, Q_SORTED, BELOW, UPTO, HERE = 0, 32, 48, 64, 80, 96


def ranked(values):
    n = values.shape[0]
    rank = jnp.sum((values[None, :] < values[:, None]).astype(jnp.int32), axis=1)
    hit = rank[:, None] == jnp.arange(n)[None, :]
    index = jnp.sum(jnp.where(hit, jnp.arange(n)[:, None], 0), axis=0)
    return index, jnp.sum(jnp.where(hit, values[:, None], 0), axis=0)


def plan(span_order, place):
    order = span_order.reshape(4, 4, 4, 2)
    x_is = place["x"] == jnp.arange(4)
    far = place["z2"] * 2 + place["z1"] == jnp.arange(4)
    half = place["y2"] == jnp.arange(2)
    keys = jnp.sum(jnp.where(x_is[:, None], order, 0), axis=2).reshape(K_SPANS)
    mine = far[:, None, None, None] & half
    queries = jnp.sum(jnp.where(mine, order, 0), axis=(0, 3))
    source = (place["x"] - jnp.arange(4)) % 4
    picked = source[:, None] == jnp.arange(4)
    queries = jnp.sum(jnp.where(picked[:, None, :], queries[None], 0), axis=2)
    queries = queries.reshape(Q_UNITS)
    k_index, k_sorted = ranked(keys)
    q_index, q_sorted = ranked(queries)
    below = jnp.sum((k_sorted[None, :] < q_sorted[:, None]).astype(jnp.int32), axis=1)
    upto = jnp.sum((k_sorted[None, :] <= q_sorted[:, None]).astype(jnp.int32), axis=1)
    here = jnp.full((Q_UNITS,), place["core"] * 4 + place["x"], jnp.int32)
    scalars = jnp.concatenate([k_index, q_index, q_sorted, below, upto, here])
    row = jnp.arange(SPAN, dtype=jnp.int32)
    core = jnp.where(row < UNIT, place["core"], 1 - place["core"])
    within = row % UNIT
    offset = core * QUARTER + within + (within // QUARTER) * QUARTER
    columns = k_sorted[:, None] * SPAN + offset[None, :]
    return scalars.astype(jnp.int32), columns.reshape(CHUNKS, 1, CHUNK).astype(jnp.int32)


def attend_kernel(
    scalars, columns, q0_ref, q1_ref, q2_ref, q3_ref, own_ref, other_ref, out_ref,
    q_ref, sorted_kv, keys_t, values, q_group, q_position, scores, top, total, stats,
):
    for block, block_ref in enumerate((q0_ref, q1_ref, q2_ref, q3_ref)):
        q_ref[block * BLOCK_ROWS : (block + 1) * BLOCK_ROWS, :] = block_ref[...]

    def place(rank, _):
        source = pl.multiple_of(scalars[K_INDEX + rank] * UNIT, UNIT)
        for half, kv_ref in enumerate((own_ref, other_ref)):
            target = pl.ds(pl.multiple_of((2 * rank + half) * UNIT, UNIT), UNIT)
            sorted_kv[target, :] = kv_ref[pl.ds(source, UNIT), :]
        return 0

    lax.fori_loop(0, K_SPANS, place, 0)
    for chunk in range(CHUNKS):
        rows = slice(chunk * CHUNK, (chunk + 1) * CHUNK)
        keys_t[chunk] = sorted_kv[rows, :HEAD_DIM].T
        values[chunk, :, :HEAD_DIM] = sorted_kv[rows, HEAD_DIM:]
        values[chunk, :, HEAD_DIM:] = jnp.ones((CHUNK, HEAD_DIM), jnp.bfloat16)

    row = lax.broadcasted_iota(jnp.int32, (UNIT, HEAD_DIM), 0)
    offset = row + jnp.where(row >= QUARTER, QUARTER, 0) + scalars[HERE] // 4 * QUARTER
    lane = lax.broadcasted_iota(jnp.int32, (UNIT, HEAD_DIM), 1)
    part_rows = [slice(p * PART_ROWS, (p + 1) * PART_ROWS) for p in range(PARTS)]

    def run_group(group, _):
        first = group * TOGETHER
        for u in range(TOGETHER):
            source = pl.multiple_of(scalars[Q_INDEX + first + u] * UNIT, UNIT)
            position = scalars[Q_SORTED + first + u] * SPAN + offset
            for g in range(GROUP):
                to = slice((u * GROUP + g) * UNIT, (u * GROUP + g + 1) * UNIT)
                q_group[to, :] = q_ref[
                    pl.ds(source, UNIT), g * HEAD_DIM : (g + 1) * HEAD_DIM
                ]
                q_position[to, :] = position
        top[...] = jnp.full(top.shape, LOWEST, jnp.float32)
        total[...] = jnp.zeros(total.shape, jnp.float32)

        def score(chunk, masked):
            for rows in part_rows:
                block = jnp.dot(
                    q_group[rows, :], keys_t[chunk], preferred_element_type=jnp.float32
                )
                if masked:
                    position = q_position[rows, :]
                    tiles = [
                        jnp.where(
                            columns[chunk, :, t : t + HEAD_DIM] <= position,
                            block[:, t : t + HEAD_DIM],
                            LOWEST,
                        )
                        for t in range(0, CHUNK, HEAD_DIM)
                    ]
                    block = jnp.concatenate(tiles, axis=1)
                else:
                    tiles = [block[:, t : t + HEAD_DIM] for t in range(0, CHUNK, HEAD_DIM)]
                scores[chunk, rows, :] = block
                top[rows, :] = functools.reduce(jnp.maximum, tiles, top[rows, :])

        def weigh(chunk):
            for rows in part_rows:
                highest = top[rows, :]
                tiles = [
                    jnp.exp2((scores[chunk, rows, t : t + HEAD_DIM] - highest) * EXPONENT)
                    for t in range(0, CHUNK, HEAD_DIM)
                ]
                total[rows, :] += jnp.dot(
                    jnp.concatenate(tiles, axis=1).astype(jnp.bfloat16),
                    values[chunk],
                    preferred_element_type=jnp.float32,
                )

        ends = (scalars[UPTO + first + TOGETHER - 1] * SPAN + CHUNK - 1) // CHUNK
        for count in range(1, CHUNKS + 1):

            @pl.when(ends == count)
            def _():
                for chunk in range(count):
                    score(chunk, True)
                highest = jnp.max(top[...], axis=1, keepdims=True)
                top[...] = jnp.broadcast_to(highest, top.shape)
                for chunk in range(count):
                    weigh(chunk)

        for u in range(TOGETHER):
            unit = scalars[Q_INDEX + first + u]
            block, within = (scalars[HERE] - unit // 4) % 4, unit % 4
            target = block * (BLOCK_ROWS + STAT_ROWS) + within * UNIT
            target = pl.ds(pl.multiple_of(target, 16), UNIT)
            packed = jnp.zeros((UNIT, HEAD_DIM), jnp.float32)
            for g in range(GROUP):
                part = slice((u * GROUP + g) * UNIT, (u * GROUP + g + 1) * UNIT)
                weight_sum = total[part, HEAD_DIM:]
                highest = top[part, :]
                some = (highest > LOWEST) & (weight_sum > 0.0)
                safe = jnp.where(some, weight_sum, 1.0)
                out_ref[target, g * HEAD_DIM : (g + 1) * HEAD_DIM] = (
                    total[part, :HEAD_DIM] / safe
                ).astype(jnp.bfloat16)
                level = jnp.where(some, highest * EXPONENT + jnp.log2(safe), LOWEST)
                high = level.astype(jnp.bfloat16).astype(jnp.float32)
                rest = level - high
                middle = rest.astype(jnp.bfloat16).astype(jnp.float32)
                low = rest - middle
                packed = jnp.where(lane == 3 * g, high, packed)
                packed = jnp.where(lane == 3 * g + 1, middle, packed)
                packed = jnp.where(lane == 3 * g + 2, low, packed)
            target = pl.ds(pl.multiple_of(block * BLOCK_ROWS + within * UNIT, UNIT), UNIT)
            stats[target, :] = packed.astype(jnp.bfloat16)
        return 0

    lax.fori_loop(0, Q_UNITS // TOGETHER, run_group, 0)

    pick = (
        lax.broadcasted_iota(jnp.int32, (16, HEAD_DIM), 0)
        == lax.broadcasted_iota(jnp.int32, (16, HEAD_DIM), 1)
    ).astype(jnp.bfloat16)
    for block in range(Q_ROWS // BLOCK_ROWS):
        turned = lax.dot_general(
            pick,
            stats[block * BLOCK_ROWS : (block + 1) * BLOCK_ROWS, :],
            (((1,), (1,)), ((), ())),
            preferred_element_type=jnp.float32,
        ).astype(jnp.bfloat16)
        at = block * (BLOCK_ROWS + STAT_ROWS) + BLOCK_ROWS
        out_ref[at : at + STAT_ROWS, :BLOCK_ROWS] = turned
        out_ref[at : at + STAT_ROWS, BLOCK_ROWS:] = jnp.zeros(
            (STAT_ROWS, Q_COLS - BLOCK_ROWS), jnp.bfloat16
        )


def attend(scalars, columns, *arrays):
    vmem = pl.BlockSpec(memory_space=pltpu.VMEM)
    blocks = Q_ROWS // BLOCK_ROWS
    return pl.pallas_call(
        attend_kernel,
        out_shape=jax.ShapeDtypeStruct((blocks * (BLOCK_ROWS + STAT_ROWS), Q_COLS), jnp.bfloat16),
        in_specs=[pl.BlockSpec(memory_space=pltpu.SMEM)] + [vmem] * 7,
        out_specs=vmem,
        scratch_shapes=[
            pltpu.VMEM((Q_ROWS, Q_COLS), jnp.bfloat16),
            pltpu.VMEM((KEYS, 2 * HEAD_DIM), jnp.bfloat16),
            pltpu.VMEM((CHUNKS, HEAD_DIM, CHUNK), jnp.bfloat16),
            pltpu.VMEM((CHUNKS, CHUNK, 2 * HEAD_DIM), jnp.bfloat16),
            pltpu.VMEM((GROUP_ROWS, HEAD_DIM), jnp.bfloat16),
            pltpu.VMEM((GROUP_ROWS, HEAD_DIM), jnp.int32),
            pltpu.VMEM((CHUNKS, GROUP_ROWS, CHUNK), jnp.float32),
            pltpu.VMEM((GROUP_ROWS, HEAD_DIM), jnp.float32),
            pltpu.VMEM((GROUP_ROWS, 2 * HEAD_DIM), jnp.float32),
            pltpu.VMEM((Q_ROWS, HEAD_DIM), jnp.bfloat16),
        ],
        compiler_params=pltpu.CompilerParams(vmem_limit_bytes=40 * 1024 * 1024),
        cost_estimate=pl.CostEstimate(
            flops=2_400_000_000, bytes_accessed=4_000_000, transcendentals=5_000_000
        ),
        name="attend",
    )(scalars, columns, *arrays)


def combine_kernel(parts_ref, out_ref):
    parts = parts_ref.shape[0]
    row = lax.broadcasted_iota(jnp.int32, (16, Q_COLS), 0)
    head = lax.broadcasted_iota(jnp.int32, (16, Q_COLS), 1) // HEAD_DIM
    spread = ((row >= 3 * head) & (row < 3 * head + 3)).astype(jnp.bfloat16)
    levels = []
    for p in range(parts):
        turned = parts_ref[p, BLOCK_ROWS:, :BLOCK_ROWS]
        levels.append(
            lax.dot_general(
                turned,
                spread,
                (((0,), (0,)), ((), ())),
                preferred_element_type=jnp.float32,
            )
        )
    highest = functools.reduce(jnp.maximum, levels)
    shares = [jnp.exp2(level - highest) for level in levels]
    summed = sum(
        parts_ref[p, :BLOCK_ROWS, :].astype(jnp.float32) * shares[p] for p in range(parts)
    )
    out_ref[...] = (summed / sum(shares)).astype(jnp.bfloat16)


def combine(parts):
    vmem = pl.BlockSpec(memory_space=pltpu.VMEM)
    return pl.pallas_call(
        combine_kernel,
        out_shape=jax.ShapeDtypeStruct((BLOCK_ROWS, Q_COLS), jnp.bfloat16),
        in_specs=[vmem],
        out_specs=vmem,
        compiler_params=pltpu.CompilerParams(vmem_limit_bytes=8 * 1024 * 1024),
        name="combine",
    )(parts)


def exchange(blocks, axes):
    return lax.all_to_all(blocks, axes, split_axis=0, concat_axis=0, tiled=True)


def spread(blocks, axes, chosen):
    sizes = [SIZES[AXES.index(a)] for a in axes]
    lead = [n if a in chosen else 1 for a, n in zip(axes, sizes)]
    shape = blocks.shape[1:]
    blocks = jnp.broadcast_to(blocks.reshape(*lead, *shape), (*sizes, *shape))
    return blocks.reshape(math.prod(sizes), *shape)


def turn(block, axis, step):
    size = SIZES[AXES.index(axis)]
    return lax.ppermute(block, axis, [(i, (i + step) % size) for i in range(size)])


def shards(queries, keys_values, span_order):
    rows = queries.shape[0]
    scalars, columns = plan(span_order, {a: lax.axis_index(a) for a in AXES})
    by_head = jnp.transpose(queries.reshape(rows, KV_HEADS, Q_COLS), (1, 0, 2))
    mine = exchange(by_head, HEAD_AXES).reshape(BLOCK_ROWS, Q_COLS)
    own = jnp.transpose(keys_values, (1, 0, 2))
    mine, own = lax.optimization_barrier((mine, own))
    own = spread(own, KEY_AXES, HEAD_AXES)
    own = exchange(own, KEY_AXES).reshape(KEYS // 2, 2 * HEAD_DIM)
    gathered = [mine] + [turn(mine, "x", step) for step in range(1, 4)]
    own, *gathered = lax.optimization_barrier((own, *gathered))
    other = turn(own, "core", 1)
    partial = attend(scalars, columns, *gathered, own, other)
    partial = partial.reshape(4, BLOCK_ROWS + STAT_ROWS, Q_COLS)
    output = combine(exchange(partial, QUERY_AXES))
    output = exchange(output.reshape(KV_HEADS, rows, Q_COLS), HEAD_AXES)
    return jnp.transpose(output, (1, 0, 2)).reshape(rows, HEADS, HEAD_DIM)


def solution(mesh):
    fine = Mesh(mesh.devices.reshape(SIZES), AXES)
    placed = (P(AXES, None, None), P(AXES, None, None), P())
    return jax.shard_map(
        shards,
        mesh=fine,
        in_specs=placed,
        out_specs=P(AXES, None, None),
        check_vma=False,
    )
```

```python
import functools
import math

import jax
import jax.numpy as jnp
from jax import lax
from jax.experimental import pallas as pl
from jax.experimental.pallas import tpu as pltpu
from jax.sharding import Mesh, PartitionSpec as P

HEADS = 32
KV_HEADS = 8
GROUP = HEADS // KV_HEADS
HEAD_DIM = 128
SPAN = 96
QUARTER = 24
UNIT = 48
K_SPANS = 32
KEYS = K_SPANS * SPAN
Q_UNITS = 16
Q_ROWS = Q_UNITS * UNIT
TOGETHER = 4
GROUP_ROWS = TOGETHER * GROUP * UNIT
PARTS = 4
PART_ROWS = GROUP_ROWS // PARTS
CHUNK = 768
CHUNKS = KEYS // CHUNK
Q_COLS = GROUP * HEAD_DIM
BLOCK_ROWS = 192
STAT_ROWS = 16
EXPONENT = math.log2(math.e) / math.sqrt(HEAD_DIM)
LOWEST = -1e30

AXES = ("z2", "z1", "zl", "yl", "x", "y2", "y1", "core")
SIZES = (2, 2, 2, 2, 4, 2, 2, 2)
HEAD_AXES = ("zl", "yl", "y1")
QUERY_AXES = ("x",)
KEY_AXES = ("z2", "z1", "zl", "yl", "y2", "y1")

K_INDEX, Q_INDEX, Q_SORTED, BELOW, UPTO, HERE = 0, 32, 48, 64, 80, 96


def ranked(values):
    n = values.shape[0]
    rank = jnp.sum((values[None, :] < values[:, None]).astype(jnp.int32), axis=1)
    hit = rank[:, None] == jnp.arange(n)[None, :]
    index = jnp.sum(jnp.where(hit, jnp.arange(n)[:, None], 0), axis=0)
    return index, jnp.sum(jnp.where(hit, values[:, None], 0), axis=0)


def plan(span_order, place):
    order = span_order.reshape(4, 4, 4, 2)
    x_is = place["x"] == jnp.arange(4)
    far = place["z2"] * 2 + place["z1"] == jnp.arange(4)
    half = place["y2"] == jnp.arange(2)
    keys = jnp.sum(jnp.where(x_is[:, None], order, 0), axis=2).reshape(K_SPANS)
    mine = far[:, None, None, None] & half
    queries = jnp.sum(jnp.where(mine, order, 0), axis=(0, 3))
    source = (place["x"] - jnp.arange(4)) % 4
    picked = source[:, None] == jnp.arange(4)
    queries = jnp.sum(jnp.where(picked[:, None, :], queries[None], 0), axis=2)
    queries = queries.reshape(Q_UNITS)
    k_index, k_sorted = ranked(keys)
    q_index, q_sorted = ranked(queries)
    below = jnp.sum((k_sorted[None, :] < q_sorted[:, None]).astype(jnp.int32), axis=1)
    upto = jnp.sum((k_sorted[None, :] <= q_sorted[:, None]).astype(jnp.int32), axis=1)
    here = jnp.full((Q_UNITS,), place["core"] * 4 + place["x"], jnp.int32)
    scalars = jnp.concatenate([k_index, q_index, q_sorted, below, upto, here])
    row = jnp.arange(SPAN, dtype=jnp.int32)
    core = jnp.where(row < UNIT, place["core"], 1 - place["core"])
    within = row % UNIT
    offset = core * QUARTER + within + (within // QUARTER) * QUARTER
    columns = k_sorted[:, None] * SPAN + offset[None, :]
    return scalars.astype(jnp.int32), columns.reshape(CHUNKS, 1, CHUNK).astype(jnp.int32)


def attend_kernel(
    scalars, columns, q0_ref, q1_ref, q2_ref, q3_ref, own_ref, other_ref, out_ref,
    q_ref, sorted_kv, keys_t, values, q_group, q_position, scores, top, total, stats,
):
    for block, block_ref in enumerate((q0_ref, q1_ref, q2_ref, q3_ref)):
        q_ref[block * BLOCK_ROWS : (block + 1) * BLOCK_ROWS, :] = block_ref[...]

    def place(rank, _):
        source = pl.multiple_of(scalars[K_INDEX + rank] * UNIT, UNIT)
        for half, kv_ref in enumerate((own_ref, other_ref)):
            target = pl.ds(pl.multiple_of((2 * rank + half) * UNIT, UNIT), UNIT)
            sorted_kv[target, :] = kv_ref[pl.ds(source, UNIT), :]
        return 0

    lax.fori_loop(0, K_SPANS, place, 0)
    for chunk in range(CHUNKS):
        rows = slice(chunk * CHUNK, (chunk + 1) * CHUNK)
        keys_t[chunk] = sorted_kv[rows, :HEAD_DIM].T
        values[chunk, :, :HEAD_DIM] = sorted_kv[rows, HEAD_DIM:]
        values[chunk, :, HEAD_DIM:] = jnp.ones((CHUNK, HEAD_DIM), jnp.bfloat16)

    row = lax.broadcasted_iota(jnp.int32, (UNIT, HEAD_DIM), 0)
    offset = row + jnp.where(row >= QUARTER, QUARTER, 0) + scalars[HERE] // 4 * QUARTER
    lane = lax.broadcasted_iota(jnp.int32, (UNIT, HEAD_DIM), 1)
    part_rows = [slice(p * PART_ROWS, (p + 1) * PART_ROWS) for p in range(PARTS)]

    def run_group(group, _):
        first = group * TOGETHER
        for u in range(TOGETHER):
            source = pl.multiple_of(scalars[Q_INDEX + first + u] * UNIT, UNIT)
            position = scalars[Q_SORTED + first + u] * SPAN + offset
            for g in range(GROUP):
                to = slice((u * GROUP + g) * UNIT, (u * GROUP + g + 1) * UNIT)
                q_group[to, :] = q_ref[
                    pl.ds(source, UNIT), g * HEAD_DIM : (g + 1) * HEAD_DIM
                ]
                q_position[to, :] = position

        def score(chunk, masked, first_chunk):
            for rows in part_rows:
                block = jnp.dot(
                    q_group[rows, :], keys_t[chunk], preferred_element_type=jnp.float32
                )
                if masked:
                    position = q_position[rows, :]
                    tiles = [
                        jnp.where(
                            columns[chunk, :, t : t + HEAD_DIM] <= position,
                            block[:, t : t + HEAD_DIM],
                            LOWEST,
                        )
                        for t in range(0, CHUNK, HEAD_DIM)
                    ]
                    block = jnp.concatenate(tiles, axis=1)
                else:
                    tiles = [block[:, t : t + HEAD_DIM] for t in range(0, CHUNK, HEAD_DIM)]
                scores[chunk, rows, :] = block
                if not first_chunk:
                    tiles.append(top[rows, :])
                top[rows, :] = functools.reduce(jnp.maximum, tiles)

        def weigh(chunk, first_chunk):
            for rows in part_rows:
                highest = top[rows, :]
                tiles = [
                    jnp.exp2((scores[chunk, rows, t : t + HEAD_DIM] - highest) * EXPONENT)
                    for t in range(0, CHUNK, HEAD_DIM)
                ]
                product = jnp.dot(
                    jnp.concatenate(tiles, axis=1).astype(jnp.bfloat16),
                    values[chunk],
                    preferred_element_type=jnp.float32,
                )
                total[rows, :] = product if first_chunk else total[rows, :] + product

        ends = (scalars[UPTO + first + TOGETHER - 1] * SPAN + CHUNK - 1) // CHUNK
        @pl.when(ends == 0)
        def _():
            top[...] = jnp.full(top.shape, LOWEST, jnp.float32)
            total[...] = jnp.zeros(total.shape, jnp.float32)

        for count in range(1, CHUNKS + 1):

            @pl.when(ends == count)
            def _():
                for chunk in range(count):
                    score(chunk, True, chunk == 0)
                highest = jnp.max(top[...], axis=1, keepdims=True)
                top[...] = jnp.broadcast_to(highest, top.shape)
                for chunk in range(count):
                    weigh(chunk, chunk == 0)

        for u in range(TOGETHER):
            unit = scalars[Q_INDEX + first + u]
            block, within = (scalars[HERE] - unit // 4) % 4, unit % 4
            target = block * (BLOCK_ROWS + STAT_ROWS) + within * UNIT
            target = pl.ds(pl.multiple_of(target, 16), UNIT)
            tops = jnp.full((UNIT, HEAD_DIM), LOWEST, jnp.float32)
            sums = jnp.ones((UNIT, HEAD_DIM), jnp.float32)
            for g in range(GROUP):
                part = slice((u * GROUP + g) * UNIT, (u * GROUP + g + 1) * UNIT)
                weight_sum = total[part, HEAD_DIM:]
                highest = top[part, :]
                some = (highest > LOWEST) & (weight_sum > 0.0)
                safe = jnp.where(some, weight_sum, 1.0)
                out_ref[target, g * HEAD_DIM : (g + 1) * HEAD_DIM] = (
                    total[part, :HEAD_DIM] / safe
                ).astype(jnp.bfloat16)
                here = (lane // 3 == g) & some
                tops = jnp.where(here, highest, tops)
                sums = jnp.where(here, safe, sums)
            level = jnp.where(tops > LOWEST, tops * EXPONENT + jnp.log2(sums), LOWEST)
            high = level.astype(jnp.bfloat16).astype(jnp.float32)
            rest = level - high
            middle = rest.astype(jnp.bfloat16).astype(jnp.float32)
            packed = jnp.where(lane % 3 == 1, middle, rest - middle)
            packed = jnp.where(lane % 3 == 0, high, packed)
            target = pl.ds(pl.multiple_of(block * BLOCK_ROWS + within * UNIT, UNIT), UNIT)
            stats[target, :] = packed.astype(jnp.bfloat16)
        return 0

    lax.fori_loop(0, Q_UNITS // TOGETHER, run_group, 0)

    pick = (
        lax.broadcasted_iota(jnp.int32, (16, HEAD_DIM), 0)
        == lax.broadcasted_iota(jnp.int32, (16, HEAD_DIM), 1)
    ).astype(jnp.bfloat16)
    for block in range(Q_ROWS // BLOCK_ROWS):
        turned = lax.dot_general(
            pick,
            stats[block * BLOCK_ROWS : (block + 1) * BLOCK_ROWS, :],
            (((1,), (1,)), ((), ())),
            preferred_element_type=jnp.float32,
        ).astype(jnp.bfloat16)
        at = block * (BLOCK_ROWS + STAT_ROWS) + BLOCK_ROWS
        out_ref[at : at + STAT_ROWS, :BLOCK_ROWS] = turned
        out_ref[at : at + STAT_ROWS, BLOCK_ROWS:] = jnp.zeros(
            (STAT_ROWS, Q_COLS - BLOCK_ROWS), jnp.bfloat16
        )


def attend(scalars, columns, *arrays):
    vmem = pl.BlockSpec(memory_space=pltpu.VMEM)
    blocks = Q_ROWS // BLOCK_ROWS
    return pl.pallas_call(
        attend_kernel,
        out_shape=jax.ShapeDtypeStruct((blocks * (BLOCK_ROWS + STAT_ROWS), Q_COLS), jnp.bfloat16),
        in_specs=[pl.BlockSpec(memory_space=pltpu.SMEM)] + [vmem] * 7,
        out_specs=vmem,
        scratch_shapes=[
            pltpu.VMEM((Q_ROWS, Q_COLS), jnp.bfloat16),
            pltpu.VMEM((KEYS, 2 * HEAD_DIM), jnp.bfloat16),
            pltpu.VMEM((CHUNKS, HEAD_DIM, CHUNK), jnp.bfloat16),
            pltpu.VMEM((CHUNKS, CHUNK, 2 * HEAD_DIM), jnp.bfloat16),
            pltpu.VMEM((GROUP_ROWS, HEAD_DIM), jnp.bfloat16),
            pltpu.VMEM((GROUP_ROWS, HEAD_DIM), jnp.int32),
            pltpu.VMEM((CHUNKS, GROUP_ROWS, CHUNK), jnp.float32),
            pltpu.VMEM((GROUP_ROWS, HEAD_DIM), jnp.float32),
            pltpu.VMEM((GROUP_ROWS, 2 * HEAD_DIM), jnp.float32),
            pltpu.VMEM((Q_ROWS, HEAD_DIM), jnp.bfloat16),
        ],
        compiler_params=pltpu.CompilerParams(vmem_limit_bytes=40 * 1024 * 1024),
        cost_estimate=pl.CostEstimate(
            flops=2_400_000_000, bytes_accessed=4_000_000, transcendentals=5_000_000
        ),
        name="attend",
    )(scalars, columns, *arrays)


def combine_kernel(parts_ref, out_ref):
    parts = parts_ref.shape[0]
    row = lax.broadcasted_iota(jnp.int32, (16, Q_COLS), 0)
    head = lax.broadcasted_iota(jnp.int32, (16, Q_COLS), 1) // HEAD_DIM
    spread = ((row >= 3 * head) & (row < 3 * head + 3)).astype(jnp.bfloat16)
    levels = []
    for p in range(parts):
        turned = parts_ref[p, BLOCK_ROWS:, :BLOCK_ROWS]
        levels.append(
            lax.dot_general(
                turned,
                spread,
                (((0,), (0,)), ((), ())),
                preferred_element_type=jnp.float32,
            )
        )
    highest = functools.reduce(jnp.maximum, levels)
    shares = [jnp.exp2(level - highest) for level in levels]
    summed = sum(
        parts_ref[p, :BLOCK_ROWS, :].astype(jnp.float32) * shares[p] for p in range(parts)
    )
    out_ref[...] = (summed / sum(shares)).astype(jnp.bfloat16)


def combine(parts):
    vmem = pl.BlockSpec(memory_space=pltpu.VMEM)
    return pl.pallas_call(
        combine_kernel,
        out_shape=jax.ShapeDtypeStruct((BLOCK_ROWS, Q_COLS), jnp.bfloat16),
        in_specs=[vmem],
        out_specs=vmem,
        compiler_params=pltpu.CompilerParams(vmem_limit_bytes=8 * 1024 * 1024),
        name="combine",
    )(parts)


def exchange(blocks, axes):
    return lax.all_to_all(blocks, axes, split_axis=0, concat_axis=0, tiled=True)


def spread(blocks, axes, chosen):
    sizes = [SIZES[AXES.index(a)] for a in axes]
    lead = [n if a in chosen else 1 for a, n in zip(axes, sizes)]
    shape = blocks.shape[1:]
    blocks = jnp.broadcast_to(blocks.reshape(*lead, *shape), (*sizes, *shape))
    return blocks.reshape(math.prod(sizes), *shape)


def turn(block, axis, step):
    size = SIZES[AXES.index(axis)]
    return lax.ppermute(block, axis, [(i, (i + step) % size) for i in range(size)])


def shards(queries, keys_values, span_order):
    rows = queries.shape[0]
    scalars, columns = plan(span_order, {a: lax.axis_index(a) for a in AXES})
    by_head = jnp.transpose(queries.reshape(rows, KV_HEADS, Q_COLS), (1, 0, 2))
    mine = exchange(by_head, HEAD_AXES).reshape(BLOCK_ROWS, Q_COLS)
    own = jnp.transpose(keys_values, (1, 0, 2))
    mine, own = lax.optimization_barrier((mine, own))
    own = spread(own, KEY_AXES, HEAD_AXES)
    own = exchange(own, KEY_AXES).reshape(KEYS // 2, 2 * HEAD_DIM)
    gathered = [mine] + [turn(mine, "x", step) for step in range(1, 4)]
    own, *gathered = lax.optimization_barrier((own, *gathered))
    other = turn(own, "core", 1)
    partial = attend(scalars, columns, *gathered, own, other)
    partial = partial.reshape(4, BLOCK_ROWS + STAT_ROWS, Q_COLS)
    output = combine(exchange(partial, QUERY_AXES))
    output = exchange(output.reshape(KV_HEADS, rows, Q_COLS), HEAD_AXES)
    return jnp.transpose(output, (1, 0, 2)).reshape(rows, HEADS, HEAD_DIM)


def solution(mesh):
    fine = Mesh(mesh.devices.reshape(SIZES), AXES)
    placed = (P(AXES, None, None), P(AXES, None, None), P())
    return jax.shard_map(
        shards,
        mesh=fine,
        in_specs=placed,
        out_specs=P(AXES, None, None),
        check_vma=False,
    )
```
